32 devices in a mesh: dp: 4 (over y, core), row: 2 (over x), col: 4 (over z).
Axes of the slice: x: 2, y: 2, z: 4, core: 2. Of those that a mesh axis runs over, the one named last changes fastest.
Arguments:
- tokens: float32 [10240, 1024], P(('dp', 'row'), 'col'), may hold values from -6 to 6
- lengths: int32 [16, 4], P(('dp', 'col')), may hold values from 1 to 512, 640 in all within a row
- w_qkv: float32 [1024, 3, 1024], P('col', None, 'row'), may hold values from -0.1875 to 0.1875
- qv_bias: float32 [2, 1024], P(None, 'row'), may hold values from -3 to 3
- w_out: float32 [1024, 1024], P('row', 'col'), may hold values from -1.5 to 1.5
- out_bias: float32 [1024], P('col'), may hold values from -3 to 3
- w_up: float32 [1024, 4096], P('col', 'row'), may hold values from -0.1875 to 0.1875
- up_bias: float32 [4096], P('row'), may hold values from -3 to 3
- w_down: float32 [4096, 1024], P('row', 'col'), may hold values from -0.09375 to 0.09375
- down_bias: float32 [1024], P('col'), may hold values from -3 to 3
- norm_gain: float32 [2, 1024], P(None, 'col'), may hold values from 0.25 to 1.75
- norm_bias: float32 [2, 1024], P(None, 'col'), may hold values from -2 to 2
- cotangent: float32 [10240, 1024], P(('dp', 'row'), 'col'), may hold values from -6 to 6
Outputs:
- output: float32 [10240, 1024], P(('dp', 'row'), 'col')
- grad_input: float32 [10240, 1024], P(('dp', 'row'), 'col')
- grad_w_qkv: float32 [1024, 3, 1024], P('col', None, 'row')
- grad_qv_bias: float32 [2, 1024], P(None, 'row')
- grad_w_out: float32 [1024, 1024], P('row', 'col')
- grad_out_bias: float32 [1024], P('col')
- grad_w_up: float32 [1024, 4096], P('col', 'row')
- grad_up_bias: float32 [4096], P('row')
- grad_w_down: float32 [4096, 1024], P('row', 'col')
- grad_down_bias: float32 [1024], P('col')
- grad_norm_gain: float32 [2, 1024], P(None, 'col')
- grad_norm_bias: float32 [2, 1024], P(None, 'col')
The draws below stay inside these ranges and needn't reach their ends.
Inputs may be any that keep to these rules, and one draw needn't show every extreme that they name: Each row lists the lengths of the 4 sequences of one data row in order; they sum to 640.
All inputs are finite; a program needn't handle non-finite values.
Results may differ from the reference program's by a relative error of at most 0.015.
The reference program's roundings to bfloat16 on the way count: a program that leaves them out, or rounds other values in their place, can miss the bound.
Values may be sent and summed in bfloat16 or wider, within the bound.
A program may use at most 192 MiB of HBM per device.

```python
import math
import jax
import jax.numpy as jnp
import numpy as np
from jax import lax

D = 1024
H = 16
HD = 64
FF = 4096
MAXLEN = 512
NSEQ = 4
ROW_TOK = 640
ROWS = 16
TOKENS = 10240


def shard_levels(key, shape, pieces, least, top_value):
    level, own = 1.0, jax.random.fold_in(key, 6)
    for dim, blocks in pieces:
        steps = jnp.exp(jax.random.uniform(jax.random.fold_in(own, dim), (blocks,), jnp.float32, least / len(pieces), top_value / len(pieces)))
        level = level * jnp.repeat(steps, shape[dim] // blocks).reshape([-1 if axis == dim else 1 for axis in range(len(shape))])
    return level


def length_profile(count, total, reach, skew):
    weights = [(1 << 20) // math.isqrt(rank ** skew) + 1 for rank in range(2, count + 1)]
    rest, counts = total - reach - (count - 1), [1] * (count - 1)
    while rest > 0:
        candidates = [i for i in range(count - 1) if counts[i] < reach]
        whole, remaining = sum([weights[i] for i in candidates]), rest
        for i in candidates:
            addition = min(reach - counts[i], max(1, remaining * weights[i] // whole), rest)
            counts[i] = counts[i] + addition
            rest = rest - addition
    return np.array([reach] + counts)


def ragged(stream_key, amount, total, most, lean):
    if amount == 2:
        one = jax.random.randint(stream_key, (), max(1, total - most), min(most, total - 1) + 1)
        return jnp.stack([one, total - one])
    tallies = jnp.asarray(length_profile(amount, total, most, lean), jnp.int32)
    pairs = (amount - 1) // 2
    giver, sink = tallies[1:1 + 2 * pairs:2], tallies[2:2 + 2 * pairs:2]
    room = jnp.minimum(giver - 1, most - sink)
    shifted = jax.random.randint(jax.random.fold_in(stream_key, 1), (pairs,), 0, 1 << 20) % (room + 1)
    tallies = tallies.at[1:1 + 2 * pairs:2].set(giver - shifted).at[2:2 + 2 * pairs:2].set(sink + shifted)
    return tallies[jax.random.permutation(jax.random.fold_in(stream_key, 2), amount)]


def normal_values(rng, shape, scale, limit, split=(), held_as=jnp.bfloat16):
    entries = scale * jax.random.normal(rng, shape, jnp.float32)
    if split:
        entries = entries * shard_levels(rng, shape, split, -0.22, 0.18)
    return jnp.clip(entries, -limit, limit).astype(held_as)


def setup_inputs(seed: int = 0) -> dict:
    key_of = jax.random.split(jax.random.key(seed), 14)
    return {
        "tokens": normal_values(key_of[0], (TOKENS, D), 1.0, 6.0, ((0, 8), (1, 4)), jnp.float32),
        "lengths": jax.vmap(lambda own: ragged(own, NSEQ, ROW_TOK, MAXLEN, 2))(jax.random.split(key_of[1], ROWS)).reshape((ROWS, NSEQ)).astype(jnp.int32),
        "w_qkv": normal_values(key_of[2], (D, 3, D), D ** -0.5, 0.1875, ((0, 4), (2, 2)), jnp.float32),
        "qv_bias": normal_values(key_of[3], (2, D), 0.5, 3.0, ((1, 2),), jnp.float32),
        "w_out": normal_values(key_of[4], (D, D), (max(D // 64, 1)) ** -0.5, 1.5, ((0, 2), (1, 4)), jnp.float32),
        "out_bias": normal_values(key_of[5], (D,), 0.5, 3.0, ((0, 4),), jnp.float32),
        "w_up": normal_values(key_of[6], (D, FF), D ** -0.5, 0.1875, ((0, 4), (1, 2)), jnp.float32),
        "up_bias": normal_values(key_of[7], (FF,), 0.5, 3.0, ((0, 2),), jnp.float32),
        "w_down": normal_values(key_of[8], (FF, D), FF ** -0.5, 0.09375, ((0, 2), (1, 4)), jnp.float32),
        "down_bias": normal_values(key_of[9], (D,), 0.5, 3.0, ((0, 4),), jnp.float32),
        "norm_gain": jnp.clip(1.0 + 0.15 * jax.random.normal(key_of[10], (2, D), jnp.float32), 0.25, 1.75),
        "norm_bias": normal_values(key_of[11], (2, D), 0.3, 2.0, ((1, 4),), jnp.float32),
        "cotangent": normal_values(key_of[12], (TOKENS, D), 1.0, 6.0, ((0, 8), (1, 4)), jnp.float32),
    }


EPS = 1e-05
HIGH = lax.Precision.HIGHEST

@jax.custom_vjp
def low(v):
    return lax.optimization_barrier(v.astype(jnp.bfloat16)).astype(jnp.float32)

@jax.custom_vjp
def low_back(v):
    return v

def low_keep(v):
    return (low(v), None)

def low_pass(kept, grad):
    return (grad,)

def back_keep(v):
    return (v, None)

def back_low(kept, grad):
    return (low(grad),)
low.defvjp(low_keep, low_pass)
low_back.defvjp(back_keep, back_low)

def layer_norm(values, gain_row, shift_row):
    center = lax.optimization_barrier(jnp.mean(values, -1, keepdims=True))
    spread = lax.optimization_barrier(jnp.mean(values * values, -1, keepdims=True)) - center * center
    return (values - center) * lax.rsqrt(spread + EPS) * gain_row + shift_row

def attend_row(packed):
    qkv_row, segment = packed
    length = qkv_row.shape[0]
    queries = qkv_row[:, 0].reshape(length, H, HD)
    key_rows = qkv_row[:, 1].reshape(length, H, HD)
    value_rows = qkv_row[:, 2].reshape(length, H, HD)
    scores = jnp.einsum('qhe,khe->hqk', queries, key_rows, precision=HIGH) * (1.0 / math.sqrt(HD))
    scores = low_back(scores)
    same_seq = (segment[:, None] == segment[None, :])[None]
    scores = jnp.where(same_seq, scores, -1000000000.0)
    row_max = lax.optimization_barrier(jnp.max(scores, -1, keepdims=True))
    exp_scores = jnp.exp(scores - row_max)
    attn_probs = exp_scores / lax.optimization_barrier(jnp.sum(exp_scores, -1, keepdims=True))
    context = jnp.einsum('hqk,khe->qhe', low(attn_probs), value_rows, precision=HIGH)
    return context.reshape(length, H * HD)

def reference(tokens, lengths, w_qkv, qv_bias, w_out, out_bias, w_up, up_bias, w_down, down_bias, norm_gain, norm_bias, cotangent):
    row_count = lengths.shape[0]
    seq_ends = jnp.cumsum(lengths, axis=-1).astype(jnp.int32)
    positions = jnp.arange(ROW_TOK, dtype=jnp.int32)
    segment = lax.optimization_barrier(jnp.sum((positions[None, :, None] >= seq_ends[:, None, :]).astype(jnp.int32), -1)).astype(jnp.int32)

    def forward(tokens, w_qkv, qv_bias, w_out, out_bias, w_up, up_bias, w_down, down_bias, norm_gain, norm_bias):
        tokens_low = low(tokens)
        qkv = jnp.einsum('td,dsh->tsh', tokens_low, low(w_qkv), precision=HIGH)
        full_bias = jnp.stack([qv_bias[0], jnp.zeros_like(qv_bias[0]), qv_bias[1]])
        qkv = low_back(low(qkv + full_bias))
        context = lax.map(jax.checkpoint(attend_row), (qkv.reshape(row_count, ROW_TOK, 3, H * HD), segment))
        context = low_back(low(context.reshape(-1, H * HD)))
        attn_out = low_back(jnp.dot(context, low(w_out), precision=HIGH) + out_bias)
        normed_one = layer_norm(tokens + attn_out, norm_gain[0], norm_bias[0])
        pre_act = low_back(jnp.dot(low(normed_one), low(w_up), precision=HIGH) + up_bias)
        hidden = low(jax.nn.gelu(pre_act, approximate=False))
        mlp_out = low_back(jnp.dot(hidden, low(w_down), precision=HIGH) + down_bias)
        return layer_norm(normed_one + mlp_out, norm_gain[1], norm_bias[1])
    output, pullback = jax.vjp(forward, tokens, w_qkv, qv_bias, w_out, out_bias, w_up, up_bias, w_down, down_bias, norm_gain, norm_bias)
    gradients = pullback(cotangent)
    return (output, gradients[0], gradients[1], gradients[2], gradients[3], gradients[4], gradients[5], gradients[6], gradients[7], gradients[8], gradients[9], gradients[10])
```

```python
from functools import partial
import math

import jax
import jax.numpy as jnp
from jax import lax
from jax.sharding import PartitionSpec as P

HD = 64


EPS = 1e-05


def hop(values, axis, step):
    count = lax.axis_size(axis)
    return lax.ppermute(values, axis, [(i, i ^ step) for i in range(count)])


def bit_of(axis, step):
    return (lax.axis_index(axis) & step) != 0


def in_order(mine, theirs, flag, dim):
    return jnp.stack([jnp.where(flag, theirs, mine), jnp.where(flag, mine, theirs)], dim)


def gather_weight(block):
    dp_count = lax.axis_size("dp")
    col_count = lax.axis_size("col")
    depth = block.shape[0] // dp_count
    piece = lax.dynamic_slice_in_dim(block, lax.axis_index("dp") * depth, depth, 0)
    piece = piece.astype(jnp.bfloat16)
    parts = [piece] + [hop(piece, "col", k) for k in range(1, col_count)]
    step = 1
    while len(parts) > 1:
        flag = bit_of("col", step)
        parts = [in_order(parts[i], parts[i + 1], flag, 0) for i in range(0, len(parts), 2)]
        step *= 2
    held = parts[0].reshape((col_count, 1) + piece.shape)
    step = dp_count // 2
    order = []
    while step:
        order.append(step)
        step //= 2
    for step in order:
        pair = in_order(held, hop(held, "dp", step), bit_of("dp", step), 2)
        held = pair.reshape((col_count, pair.shape[1] * 2) + piece.shape)
    return held.reshape((col_count,) + block.shape)


def reduce_weight(grad):
    dp_count = lax.axis_size("dp")
    col_count = lax.axis_size("col")
    depth = grad.shape[1] // dp_count
    tail = grad.shape[2:]
    held = grad.reshape((col_count, dp_count, depth) + tail)
    step = 1
    while step < dp_count:
        pairs = held.reshape((col_count, held.shape[1] // 2, 2, depth) + tail)
        flag = bit_of("dp", step)
        keep = jnp.where(flag, pairs[:, :, 1], pairs[:, :, 0])
        give = jnp.where(flag, pairs[:, :, 0], pairs[:, :, 1]).astype(jnp.bfloat16)
        got = hop(give, "dp", step)
        held = (keep.astype(jnp.float32) + got.astype(jnp.float32)).astype(jnp.bfloat16)
        step *= 2
    held = held[:, 0]
    here = lax.axis_index("col")
    total = lax.dynamic_index_in_dim(held, here, 0, keepdims=False).astype(jnp.float32)
    for k in range(1, col_count):
        give = lax.dynamic_index_in_dim(held, here ^ k, 0, keepdims=False)
        total = total + hop(give, "col", k).astype(jnp.float32)
    out = total.astype(jnp.bfloat16)[None]
    step = dp_count // 2
    while step:
        pair = in_order(out, hop(out, "dp", step), bit_of("dp", step), 1)
        out = pair.reshape((pair.shape[0] * 2, depth) + tail)
        step //= 2
    return out.reshape((dp_count * depth,) + tail).astype(jnp.float32)


def from_others(values):
    count = lax.axis_size("row")
    return jnp.concatenate(
        [
            lax.ppermute(values, "row", [((i + k) % count, i) for i in range(count)])
            for k in range(1, count)
        ],
        0,
    )


def to_owners(others, mine):
    count = lax.axis_size("row")
    size = mine.shape[0]
    low = others.astype(jnp.bfloat16)
    for k in range(1, count):
        got = lax.ppermute(
            low[(k - 1) * size : k * size], "row", [(i, (i + k) % count) for i in range(count)]
        )
        mine = mine + got.astype(jnp.float32)
    return mine


def owner_perm(rows, cols, k):
    pairs = []
    for r in range(rows):
        for c in range(cols):
            owner = r * cols + (c ^ k)
            pairs.append((r * cols + c, (owner % rows) * cols + owner // rows))
    return pairs


def to_tokens(values):
    rows, cols = lax.axis_size("row"), lax.axis_size("col")
    size = values.shape[0] // cols
    blocks = values.reshape(cols, size, values.shape[1])
    here = lax.axis_index("col")
    own = lax.axis_index("col") * rows + lax.axis_index("row")
    got = []
    for k in range(cols):
        give = lax.dynamic_index_in_dim(blocks, here ^ k, 0, keepdims=False)
        got.append(lax.ppermute(give, ("row", "col"), owner_perm(rows, cols, k)))
    parts, step = got, 1
    while len(parts) > 1:
        flag = ((own % cols) & step) != 0
        parts = [
            jnp.concatenate(
                [
                    jnp.where(flag, parts[i + 1], parts[i]),
                    jnp.where(flag, parts[i], parts[i + 1]),
                ],
                1,
            )
            for i in range(0, len(parts), 2)
        ]
        step *= 2
    return parts[0]


def from_tokens(values):
    rows, cols = lax.axis_size("row"), lax.axis_size("col")
    size, width = values.shape[0], values.shape[1] // cols
    own = lax.axis_index("col") * rows + lax.axis_index("row")
    got = []
    for k in range(cols):
        start = ((own % cols) ^ k) * width
        give = lax.dynamic_slice_in_dim(values, start, width, 1)
        back = [(there, here) for here, there in owner_perm(rows, cols, k)]
        got.append(lax.ppermute(give, ("row", "col"), back))
    parts, step = got, 1
    while len(parts) > 1:
        flag = bit_of("col", step)
        parts = [
            in_order(parts[i], parts[i + 1], flag, 0).reshape((-1, width))
            for i in range(0, len(parts), 2)
        ]
        step *= 2
    return parts[0]


def norm_forward(values, gain_row, shift_row):
    center = jnp.mean(values, -1, keepdims=True)
    spread = jnp.mean(values * values, -1, keepdims=True) - center * center
    inv_std = lax.rsqrt(spread + EPS)
    normal = (values - center) * inv_std
    return (normal * gain_row + shift_row, normal, inv_std)


def norm_backward(grad_out, normal, inv_std, gain_row):
    scaled = grad_out * gain_row
    first = jnp.mean(scaled, -1, keepdims=True)
    second = jnp.mean(scaled * normal, -1, keepdims=True)
    return inv_std * (scaled - first - normal * second)


def dot(first, second):
    return jnp.dot(first, second, preferred_element_type=jnp.float32)


def dot_back(first, second):
    return jnp.einsum("tf,df->td", first, second, preferred_element_type=jnp.float32)


def outer(first, second):
    return jnp.einsum("td,tf->df", first, second, preferred_element_type=jnp.float32)


def masked_scores(query_rows, key_rows, same_seq, score_scale):
    scores = (
        jnp.einsum("qhe,khe->hqk", query_rows, key_rows, preferred_element_type=jnp.float32)
        * score_scale
    )
    return jnp.where(same_seq, scores, -1000000000.0)


def attend(query_rows, key_rows, value_rows, same_seq, score_scale):
    scores = masked_scores(query_rows, key_rows, same_seq, score_scale)
    row_max = jnp.max(scores, -1, keepdims=True)
    exp_scores = jnp.exp(scores - row_max)
    totals = jnp.sum(exp_scores, -1, keepdims=True)
    attn_probs = (exp_scores / totals).astype(jnp.bfloat16)
    context = jnp.einsum("hqk,khe->qhe", attn_probs, value_rows, preferred_element_type=jnp.float32)
    return (context, row_max + jnp.log(totals))


def attend_back(query_rows, key_rows, value_rows, same_seq, score_scale, log_total, grad_context):
    scores = masked_scores(query_rows, key_rows, same_seq, score_scale)
    attn_probs = jnp.exp(scores - log_total)
    grad_probs = jnp.einsum(
        "qhe,khe->hqk", grad_context, value_rows, preferred_element_type=jnp.float32
    )
    grad_values = jnp.einsum(
        "hqk,qhe->khe",
        attn_probs.astype(jnp.bfloat16),
        grad_context,
        preferred_element_type=jnp.float32,
    )
    inner_sum = jnp.sum(attn_probs * grad_probs, -1, keepdims=True)
    grad_scores = (attn_probs * (grad_probs - inner_sum)).astype(jnp.bfloat16)
    grad_queries = (
        jnp.einsum("hqk,khe->qhe", grad_scores, key_rows, preferred_element_type=jnp.float32)
        * score_scale
    )
    grad_keys = (
        jnp.einsum("hqk,qhe->khe", grad_scores, query_rows, preferred_element_type=jnp.float32)
        * score_scale
    )
    return (grad_queries, grad_keys, grad_values)


def shards(
    tokens,
    lengths,
    w_qkv,
    qv_bias,
    w_out,
    out_bias,
    w_up,
    up_bias,
    w_down,
    down_bias,
    norm_gain,
    norm_bias,
    cotangent,
):
    score_scale = 1.0 / math.sqrt(HD)
    gelu_exact = partial(jax.nn.gelu, approximate=False)
    rows, cols = lax.axis_size("row"), lax.axis_size("col")
    here_row, here_col = lax.axis_index("row"), lax.axis_index("col")
    own_tokens = to_tokens(tokens)
    own_low = own_tokens.astype(jnp.bfloat16)
    other_low = from_others(own_low)
    wide = w_qkv.shape[2]
    w_qkv_all = gather_weight(w_qkv.reshape(w_qkv.shape[0], 3 * wide)).reshape(-1, 3 * wide)
    w_out_all = gather_weight(w_out).transpose(1, 0, 2).reshape(w_out.shape[0], -1)
    w_up_all = gather_weight(w_up).reshape(-1, w_up.shape[1])
    w_down_all = gather_weight(w_down).transpose(1, 0, 2).reshape(w_down.shape[0], -1)
    own_cotangent = to_tokens(cotangent)
    small = jnp.concatenate([out_bias, down_bias, norm_gain[0], norm_gain[1], norm_bias[0], norm_bias[1]])
    small = lax.all_gather(small, "col", axis=0).reshape(cols, 6, -1)
    small = small.transpose(1, 0, 2).reshape(6, -1)
    out_bias_all, down_bias_all = small[0], small[1]
    gains, shifts = small[2:4], small[4:6]

    size = own_low.shape[0]
    full_bias = jnp.concatenate([qv_bias[0], jnp.zeros_like(qv_bias[0]), qv_bias[1]])
    qkv = jnp.concatenate(
        [
            (dot(own_low, w_qkv_all) + full_bias).astype(jnp.bfloat16),
            (dot(other_low, w_qkv_all) + full_bias).astype(jnp.bfloat16),
        ],
        0,
    )
    length = qkv.shape[0]
    head_count = wide // HD
    qkv = qkv.reshape(length, 3, head_count, HD)
    query_rows, key_rows, value_rows = qkv[:, 0], qkv[:, 1], qkv[:, 2]
    seq_ends = jnp.cumsum(lengths[0])
    positions = (jnp.arange(length, dtype=jnp.int32) + here_row * size) % length
    segment = jnp.sum((positions[:, None] >= seq_ends[None, :]).astype(jnp.int32), -1)
    same_seq = (segment[:, None] == segment[None, :])[None]
    context, log_total = attend(query_rows, key_rows, value_rows, same_seq, score_scale)
    context = context.reshape(length, wide).astype(jnp.bfloat16)
    attn_other = dot(context[size:], w_out_all)
    attn_out = to_owners(attn_other, dot(context[:size], w_out_all)) + out_bias_all
    normed_one, normal_one, inv_one = norm_forward(own_tokens + attn_out, gains[0], shifts[0])
    normed_own = normed_one.astype(jnp.bfloat16)
    normed_other = from_others(normed_own)
    pre_own = dot(normed_own, w_up_all) + up_bias
    pre_other = dot(normed_other, w_up_all) + up_bias
    hidden_own = gelu_exact(pre_own).astype(jnp.bfloat16)
    hidden_other = gelu_exact(pre_other).astype(jnp.bfloat16)
    mlp_other = dot(hidden_other, w_down_all)
    mlp_out = to_owners(mlp_other, dot(hidden_own, w_down_all)) + down_bias_all
    last, normal_two, inv_two = norm_forward(normed_one + mlp_out, gains[1], shifts[1])
    output = from_tokens(last)
    grad_last = norm_backward(own_cotangent, normal_two, inv_two, gains[1])
    gain_two = jnp.sum(own_cotangent * normal_two, 0)
    shift_two = jnp.sum(own_cotangent, 0)
    mlp_grad_own = grad_last.astype(jnp.bfloat16)
    mlp_grad_other = from_others(mlp_grad_own)
    down_total = jnp.sum(mlp_grad_own, 0, dtype=jnp.float32)
    pre_grad_own = jax.vjp(gelu_exact, pre_own)[1](dot_back(mlp_grad_own, w_down_all))[0]
    pre_grad_own = pre_grad_own.astype(jnp.bfloat16)
    pre_grad_other = jax.vjp(gelu_exact, pre_other)[1](dot_back(mlp_grad_other, w_down_all))[0]
    pre_grad_other = pre_grad_other.astype(jnp.bfloat16)
    normed_part = dot_back(pre_grad_other, w_up_all)
    grad_normed = to_owners(normed_part, dot_back(pre_grad_own, w_up_all)) + grad_last
    pre_grad = jnp.concatenate([pre_grad_own, pre_grad_other], 0)
    up_total = jnp.sum(pre_grad, 0, dtype=jnp.float32)
    down_grad = outer(
        jnp.concatenate([hidden_own, hidden_other], 0),
        jnp.concatenate([mlp_grad_own, mlp_grad_other], 0),
    )
    down_grad = down_grad.astype(jnp.bfloat16).reshape(w_down.shape[0], cols, -1).transpose(1, 0, 2)
    grad_w_down = reduce_weight(down_grad)
    up_grad = outer(jnp.concatenate([normed_own, normed_other], 0), pre_grad).astype(jnp.bfloat16)
    grad_w_up = reduce_weight(up_grad.reshape((cols,) + w_up.shape))
    grad_middle = norm_backward(grad_normed, normal_one, inv_one, gains[0])
    gain_one = jnp.sum(grad_normed * normal_one, 0)
    shift_one = jnp.sum(grad_normed, 0)
    attn_grad_own = grad_middle.astype(jnp.bfloat16)
    attn_grad_other = from_others(attn_grad_own)
    out_total = jnp.sum(attn_grad_own, 0, dtype=jnp.float32)
    grad_context = jnp.concatenate(
        [
            dot_back(attn_grad_own, w_out_all).astype(jnp.bfloat16),
            dot_back(attn_grad_other, w_out_all).astype(jnp.bfloat16),
        ],
        0,
    ).reshape(length, head_count, HD)
    out_grad = outer(context, jnp.concatenate([attn_grad_own, attn_grad_other], 0))
    out_grad = out_grad.astype(jnp.bfloat16).reshape(w_out.shape[0], cols, -1).transpose(1, 0, 2)
    grad_w_out = reduce_weight(out_grad)
    grad_queries, grad_keys, grad_values = attend_back(
        query_rows, key_rows, value_rows, same_seq, score_scale, log_total, grad_context
    )
    grad_qkv = (
        jnp.stack([grad_queries, grad_keys, grad_values], 1)
        .reshape(length, 3 * wide)
        .astype(jnp.bfloat16)
    )
    qkv_totals = jnp.sum(grad_qkv, 0, dtype=jnp.float32)
    qkv_grad = outer(jnp.concatenate([own_low, other_low], 0), grad_qkv).astype(jnp.bfloat16)
    grad_w_qkv = reduce_weight(qkv_grad.reshape(cols, -1, 3 * wide)).reshape(w_qkv.shape)
    input_other = dot_back(grad_qkv[size:], w_qkv_all)
    grad_own = to_owners(input_other, dot_back(grad_qkv[:size], w_qkv_all)) + grad_middle
    grad_input = from_tokens(grad_own)

    everywhere = lax.psum(
        jnp.stack([out_total, down_total, gain_one, gain_two, shift_one, shift_two]),
        ("dp", "row", "col"),
    )
    part = everywhere.shape[1] // cols
    mine = lax.dynamic_slice_in_dim(everywhere, here_col * part, part, 1)
    halves = lax.psum(
        jnp.concatenate([up_total, qkv_totals[:wide], qkv_totals[2 * wide :]]), ("dp", "col")
    )
    hid = up_total.shape[0]
    return (
        output,
        grad_input,
        grad_w_qkv,
        halves[hid:].reshape(2, wide),
        grad_w_out,
        mine[0],
        grad_w_up,
        halves[:hid],
        grad_w_down,
        mine[1],
        mine[2:4],
        mine[4:6],
    )


def solution(mesh):
    placed = (
        P(("dp", "row"), "col"),
        P(("dp", "col"), None),
        P("col", None, "row"),
        P(None, "row"),
        P("row", "col"),
        P("col"),
        P("col", "row"),
        P("row"),
        P("row", "col"),
        P("col"),
        P(None, "col"),
        P(None, "col"),
        P(("dp", "row"), "col"),
    )
    return jax.shard_map(
        shards,
        mesh=mesh,
        in_specs=placed,
        out_specs=(
            P(("dp", "row"), "col"),
            P(("dp", "row"), "col"),
            P("col", None, "row"),
            P(None, "row"),
            P("row", "col"),
            P("col"),
            P("col", "row"),
            P("row"),
            P("row", "col"),
            P("col"),
            P(None, "col"),
            P(None, "col"),
        ),
        check_vma=False,
    )
```

```python
from functools import partial
import math

import jax
import jax.numpy as jnp
from jax import lax
from jax.sharding import PartitionSpec as P

HD = 64


EPS = 1e-05


def hop(values, axis, step):
    count = lax.axis_size(axis)
    return lax.ppermute(values, axis, [(i, i ^ step) for i in range(count)])


def bit_of(axis, step):
    return (lax.axis_index(axis) & step) != 0


def in_order(mine, theirs, flag, dim):
    return jnp.stack([jnp.where(flag, theirs, mine), jnp.where(flag, mine, theirs)], dim)


def after(done, values):
    return lax.optimization_barrier((done, values))


def cut_piece(block):
    depth = block.shape[0] // lax.axis_size("dp")
    piece = lax.dynamic_slice_in_dim(block, lax.axis_index("dp") * depth, depth, 0)
    return piece.astype(jnp.bfloat16)


def gather_col(piece):
    col_count = lax.axis_size("col")
    parts = [piece] + [hop(piece, "col", k) for k in range(1, col_count)]
    step = 1
    while len(parts) > 1:
        flag = bit_of("col", step)
        parts = [in_order(parts[i], parts[i + 1], flag, 0) for i in range(0, len(parts), 2)]
        step *= 2
    return parts[0].reshape((col_count, 1) + piece.shape)


def gather_dp(held, step):
    if step == 0:
        return held
    pair = in_order(held, hop(held, "dp", step), bit_of("dp", step), 2)
    return pair.reshape((held.shape[0], held.shape[1] * 2) + held.shape[2:])


def whole_block(held):
    return held.reshape((held.shape[0], held.shape[1] * held.shape[2]) + held.shape[3:])


def cut_grad(grad):
    dp_count = lax.axis_size("dp")
    return grad.reshape((grad.shape[0], dp_count, grad.shape[1] // dp_count) + grad.shape[2:])


def halve_dp(held, step):
    pairs = held.reshape((held.shape[0], held.shape[1] // 2, 2) + held.shape[2:])
    flag = bit_of("dp", step)
    keep = jnp.where(flag, pairs[:, :, 1], pairs[:, :, 0])
    give = jnp.where(flag, pairs[:, :, 0], pairs[:, :, 1])
    got = hop(give, "dp", step)
    return (keep.astype(jnp.float32) + got.astype(jnp.float32)).astype(jnp.bfloat16)


def scatter_col(held):
    here = lax.axis_index("col")
    total = lax.dynamic_index_in_dim(held, here, 0, keepdims=False).astype(jnp.float32)
    for k in range(1, held.shape[0]):
        give = lax.dynamic_index_in_dim(held, here ^ k, 0, keepdims=False)
        total = total + hop(give, "col", k).astype(jnp.float32)
    return total.astype(jnp.bfloat16)[None]


def add_up(values, axes):
    for axis in axes:
        step = 1
        while step < lax.axis_size(axis):
            values = values + hop(values, axis, step)
            step *= 2
    return values


def from_others(values):
    count = lax.axis_size("row")
    return jnp.concatenate(
        [
            lax.ppermute(values, "row", [((i + k) % count, i) for i in range(count)])
            for k in range(1, count)
        ],
        0,
    )


def to_owners(others, mine):
    count = lax.axis_size("row")
    size = mine.shape[0]
    low = others.astype(jnp.bfloat16)
    for k in range(1, count):
        got = lax.ppermute(
            low[(k - 1) * size : k * size], "row", [(i, (i + k) % count) for i in range(count)]
        )
        mine = mine + got.astype(jnp.float32)
    return mine


def owner_perm(rows, cols, k):
    pairs = []
    for r in range(rows):
        for c in range(cols):
            owner = r * cols + (c ^ k)
            pairs.append((r * cols + c, (owner % rows) * cols + owner // rows))
    return pairs


def to_tokens(values):
    rows, cols = lax.axis_size("row"), lax.axis_size("col")
    size = values.shape[0] // cols
    blocks = values.reshape(cols, size, values.shape[1])
    here = lax.axis_index("col")
    own = lax.axis_index("col") * rows + lax.axis_index("row")
    got = []
    for k in range(cols):
        give = lax.dynamic_index_in_dim(blocks, here ^ k, 0, keepdims=False)
        got.append(lax.ppermute(give, ("row", "col"), owner_perm(rows, cols, k)))
    parts, step = got, 1
    while len(parts) > 1:
        flag = ((own % cols) & step) != 0
        parts = [
            jnp.concatenate(
                [
                    jnp.where(flag, parts[i + 1], parts[i]),
                    jnp.where(flag, parts[i], parts[i + 1]),
                ],
                1,
            )
            for i in range(0, len(parts), 2)
        ]
        step *= 2
    return parts[0]


def from_tokens(values):
    rows, cols = lax.axis_size("row"), lax.axis_size("col")
    size, width = values.shape[0], values.shape[1] // cols
    own = lax.axis_index("col") * rows + lax.axis_index("row")
    got = []
    for k in range(cols):
        start = ((own % cols) ^ k) * width
        give = lax.dynamic_slice_in_dim(values, start, width, 1)
        back = [(there, here) for here, there in owner_perm(rows, cols, k)]
        got.append(lax.ppermute(give, ("row", "col"), back))
    parts, step = got, 1
    while len(parts) > 1:
        flag = bit_of("col", step)
        parts = [
            in_order(parts[i], parts[i + 1], flag, 0).reshape((-1, width))
            for i in range(0, len(parts), 2)
        ]
        step *= 2
    return parts[0]


def gather_small(values):
    parts, step = values, 1
    while step < lax.axis_size("col"):
        pair = in_order(parts, hop(parts, "col", step), bit_of("col", step), 1)
        parts = pair.reshape(values.shape[0], -1)
        step *= 2
    return parts


def outer_blocks(first, second):
    width = second.shape[1] // lax.axis_size("col")
    return jnp.stack(
        [
            outer(first, second[:, i * width : (i + 1) * width]).astype(jnp.bfloat16)
            for i in range(lax.axis_size("col"))
        ]
    )


def norm_forward(values, gain_row, shift_row):
    center = jnp.mean(values, -1, keepdims=True)
    spread = jnp.mean(values * values, -1, keepdims=True) - center * center
    inv_std = lax.rsqrt(spread + EPS)
    normal = (values - center) * inv_std
    return (normal * gain_row + shift_row, normal, inv_std)


def norm_backward(grad_out, normal, inv_std, gain_row):
    scaled = grad_out * gain_row
    first = jnp.mean(scaled, -1, keepdims=True)
    second = jnp.mean(scaled * normal, -1, keepdims=True)
    return inv_std * (scaled - first - normal * second)


def dot(first, second):
    return jnp.dot(first, second, preferred_element_type=jnp.float32)


def dot_back(first, second):
    return jnp.einsum("tf,df->td", first, second, preferred_element_type=jnp.float32)


def outer(first, second):
    return jnp.einsum("td,tf->df", first, second, preferred_element_type=jnp.float32)


def masked_scores(query_rows, key_rows, same_seq, score_scale):
    scores = (
        jnp.einsum("qhe,khe->hqk", query_rows, key_rows, preferred_element_type=jnp.float32)
        * score_scale
    )
    return jnp.where(same_seq, scores, -1000000000.0)


def attend(query_rows, key_rows, value_rows, same_seq, score_scale):
    scores = masked_scores(query_rows, key_rows, same_seq, score_scale)
    row_max = jnp.max(scores, -1, keepdims=True)
    exp_scores = jnp.exp(scores - row_max)
    totals = jnp.sum(exp_scores, -1, keepdims=True)
    attn_probs = (exp_scores / totals).astype(jnp.bfloat16)
    context = jnp.einsum("hqk,khe->qhe", attn_probs, value_rows, preferred_element_type=jnp.float32)
    return (context, row_max + jnp.log(totals))


def attend_back(query_rows, key_rows, value_rows, same_seq, score_scale, log_total, grad_context):
    scores = masked_scores(query_rows, key_rows, same_seq, score_scale)
    attn_probs = jnp.exp(scores - log_total)
    grad_probs = jnp.einsum(
        "qhe,khe->hqk", grad_context, value_rows, preferred_element_type=jnp.float32
    )
    grad_values = jnp.einsum(
        "hqk,qhe->khe",
        attn_probs.astype(jnp.bfloat16),
        grad_context,
        preferred_element_type=jnp.float32,
    )
    inner_sum = jnp.sum(attn_probs * grad_probs, -1, keepdims=True)
    grad_scores = (attn_probs * (grad_probs - inner_sum)).astype(jnp.bfloat16)
    grad_queries = (
        jnp.einsum("hqk,khe->qhe", grad_scores, key_rows, preferred_element_type=jnp.float32)
        * score_scale
    )
    grad_keys = (
        jnp.einsum("hqk,qhe->khe", grad_scores, query_rows, preferred_element_type=jnp.float32)
        * score_scale
    )
    return (grad_queries, grad_keys, grad_values)


def shards(
    tokens,
    lengths,
    w_qkv,
    qv_bias,
    w_out,
    out_bias,
    w_up,
    up_bias,
    w_down,
    down_bias,
    norm_gain,
    norm_bias,
    cotangent,
):
    score_scale = 1.0 / math.sqrt(HD)
    gelu_exact = partial(jax.nn.gelu, approximate=False)
    rows, cols = lax.axis_size("row"), lax.axis_size("col")
    here_row, here_col = lax.axis_index("row"), lax.axis_index("col")
    wide = w_qkv.shape[2]
    far, near = lax.axis_size("dp") // 2, 1
    qkv_held = gather_col(cut_piece(w_qkv.reshape(w_qkv.shape[0], 3 * wide)))
    own_tokens = to_tokens(tokens)
    small = jnp.stack(
        [out_bias, down_bias, norm_gain[0], norm_gain[1], norm_bias[0], norm_bias[1]]
    )
    small = gather_small(small)
    qkv_held, (piece_out, piece_up) = after(qkv_held, (cut_piece(w_out), cut_piece(w_up)))
    out_held, up_held = gather_col(piece_out), gather_col(piece_up)
    own_low = own_tokens.astype(jnp.bfloat16)
    other_low = from_others(own_low)
    qkv_held, piece_down = after(gather_dp(qkv_held, far), cut_piece(w_down))
    down_held = gather_col(piece_down)
    qkv_held, (out_held, up_held) = after(gather_dp(qkv_held, near), (out_held, up_held))
    w_qkv_all = whole_block(qkv_held).reshape(-1, 3 * wide)
    out_held, up_held = gather_dp(out_held, far), gather_dp(up_held, far)
    out_bias_all, down_bias_all = small[0], small[1]
    gains, shifts = small[2:4], small[4:6]

    size = own_low.shape[0]
    full_bias = jnp.concatenate([qv_bias[0], jnp.zeros_like(qv_bias[0]), qv_bias[1]])
    qkv = jnp.concatenate(
        [
            (dot(own_low, w_qkv_all) + full_bias).astype(jnp.bfloat16),
            (dot(other_low, w_qkv_all) + full_bias).astype(jnp.bfloat16),
        ],
        0,
    )
    qkv, (out_held, up_held, down_held) = after(qkv, (out_held, up_held, down_held))
    out_held, down_held = gather_dp(out_held, near), gather_dp(down_held, far)
    up_held = gather_dp(up_held, near)
    length = qkv.shape[0]
    head_count = wide // HD
    qkv = qkv.reshape(length, 3, head_count, HD)
    query_rows, key_rows, value_rows = qkv[:, 0], qkv[:, 1], qkv[:, 2]
    seq_ends = jnp.cumsum(lengths[0])
    positions = (jnp.arange(length, dtype=jnp.int32) + here_row * size) % length
    segment = jnp.sum((positions[:, None] >= seq_ends[None, :]).astype(jnp.int32), -1)
    same_seq = (segment[:, None] == segment[None, :])[None]
    context, log_total = attend(query_rows, key_rows, value_rows, same_seq, score_scale)
    context = context.reshape(length, wide).astype(jnp.bfloat16)
    context, (down_held, cotangent) = after(context, (down_held, cotangent))
    w_out_all = whole_block(out_held).transpose(1, 0, 2).reshape(w_out.shape[0], -1)
    down_held = gather_dp(down_held, near)
    attn_other = dot(context[size:], w_out_all)
    attn_out = to_owners(attn_other, dot(context[:size], w_out_all)) + out_bias_all
    normed_one, normal_one, inv_one = norm_forward(own_tokens + attn_out, gains[0], shifts[0])
    normed_own = normed_one.astype(jnp.bfloat16)
    normed_own, cotangent = after(normed_own, cotangent)
    normed_other = from_others(normed_own)
    own_cotangent = to_tokens(cotangent)
    w_up_all = whole_block(up_held).reshape(-1, w_up.shape[1])
    w_down_all = whole_block(down_held).transpose(1, 0, 2).reshape(w_down.shape[0], -1)
    pre_own = dot(normed_own, w_up_all) + up_bias
    pre_other = dot(normed_other, w_up_all) + up_bias
    hidden_own = gelu_exact(pre_own).astype(jnp.bfloat16)
    hidden_other = gelu_exact(pre_other).astype(jnp.bfloat16)
    hidden = jnp.concatenate([hidden_own, hidden_other], 0)
    mlp_other = dot(hidden_other, w_down_all)
    mlp_out = to_owners(mlp_other, dot(hidden_own, w_down_all)) + down_bias_all
    last, normal_two, inv_two = norm_forward(normed_one + mlp_out, gains[1], shifts[1])
    grad_last = norm_backward(own_cotangent, normal_two, inv_two, gains[1])
    gain_two = jnp.sum(own_cotangent * normal_two, 0)
    shift_two = jnp.sum(own_cotangent, 0)
    mlp_grad_own = grad_last.astype(jnp.bfloat16)
    mlp_grad_other = from_others(mlp_grad_own)
    down_total = jnp.sum(mlp_grad_own, 0, dtype=jnp.float32)
    mlp_grad_own, last = after(mlp_grad_own, last)
    output = from_tokens(last)
    down_sum = cut_grad(outer_blocks(hidden, jnp.concatenate([mlp_grad_own, mlp_grad_other], 0)))
    down_sum = halve_dp(down_sum, near)
    pre_grad_own = jax.vjp(gelu_exact, pre_own)[1](dot_back(mlp_grad_own, w_down_all))[0]
    pre_grad_own = pre_grad_own.astype(jnp.bfloat16)
    pre_grad_other = jax.vjp(gelu_exact, pre_other)[1](dot_back(mlp_grad_other, w_down_all))[0]
    pre_grad_other = pre_grad_other.astype(jnp.bfloat16)
    pre_grad_other, down_sum = after(pre_grad_other, down_sum)
    down_sum = halve_dp(down_sum, far)
    normed_part = dot_back(pre_grad_other, w_up_all)
    grad_normed = to_owners(normed_part, dot_back(pre_grad_own, w_up_all)) + grad_last
    pre_grad = jnp.concatenate([pre_grad_own, pre_grad_other], 0)
    up_total = jnp.sum(pre_grad, 0, dtype=jnp.float32)
    up_grad = outer(jnp.concatenate([normed_own, normed_other], 0), pre_grad).astype(jnp.bfloat16)
    up_sum = halve_dp(cut_grad(up_grad.reshape((cols,) + w_up.shape)), near)
    grad_middle = norm_backward(grad_normed, normal_one, inv_one, gains[0])
    gain_one = jnp.sum(grad_normed * normal_one, 0)
    shift_one = jnp.sum(grad_normed, 0)
    attn_grad_own = grad_middle.astype(jnp.bfloat16)
    attn_grad_own, (down_sum, up_sum) = after(attn_grad_own, (down_sum, up_sum))
    attn_grad_other = from_others(attn_grad_own)
    down_sum = scatter_col(down_sum)
    up_sum = halve_dp(up_sum, far)
    out_total = jnp.sum(attn_grad_own, 0, dtype=jnp.float32)
    totals = add_up(
        jnp.stack([out_total, down_total, gain_one, gain_two, shift_one, shift_two]),
        ("row", "col", "dp"),
    )
    grad_context = jnp.concatenate(
        [
            dot_back(attn_grad_own, w_out_all).astype(jnp.bfloat16),
            dot_back(attn_grad_other, w_out_all).astype(jnp.bfloat16),
        ],
        0,
    ).reshape(length, head_count, HD)
    attn_grad = jnp.concatenate([attn_grad_own, attn_grad_other], 0)
    out_sum = halve_dp(cut_grad(outer_blocks(context, attn_grad)), near)
    grad_queries, grad_keys, grad_values = attend_back(
        query_rows, key_rows, value_rows, same_seq, score_scale, log_total, grad_context
    )
    grad_qkv = (
        jnp.stack([grad_queries, grad_keys, grad_values], 1)
        .reshape(length, 3 * wide)
        .astype(jnp.bfloat16)
    )
    grad_qkv, (down_sum, up_sum, out_sum) = after(grad_qkv, (down_sum, up_sum, out_sum))
    qkv_totals = jnp.sum(grad_qkv, 0, dtype=jnp.float32)
    qkv_grad = outer(jnp.concatenate([own_low, other_low], 0), grad_qkv).astype(jnp.bfloat16)
    qkv_sum = halve_dp(cut_grad(qkv_grad.reshape(cols, -1, 3 * wide)), near)
    out_sum = halve_dp(out_sum, far)
    up_sum = scatter_col(up_sum)
    down_sum = gather_dp(down_sum, far)
    input_other = dot_back(grad_qkv[size:], w_qkv_all)
    halves = add_up(
        jnp.concatenate([up_total, qkv_totals[:wide], qkv_totals[2 * wide :]])[None],
        ("col", "dp"),
    )[0]
    grad_own = to_owners(input_other, dot_back(grad_qkv[:size], w_qkv_all)) + grad_middle
    qkv_sum, (out_sum, up_sum, down_sum, grad_own) = after(
        qkv_sum, (out_sum, up_sum, down_sum, grad_own)
    )
    qkv_sum = halve_dp(qkv_sum, far)
    grad_input = from_tokens(grad_own)
    out_sum = scatter_col(out_sum)
    up_sum = gather_dp(up_sum, far)
    down_sum = gather_dp(down_sum, near)
    qkv_sum, (out_sum, up_sum) = after(qkv_sum, (out_sum, up_sum))
    qkv_sum = scatter_col(qkv_sum)
    out_sum = gather_dp(out_sum, far)
    up_sum = gather_dp(up_sum, near)
    qkv_sum, out_sum = after(qkv_sum, out_sum)
    qkv_sum = gather_dp(qkv_sum, far)
    out_sum = gather_dp(out_sum, near)
    qkv_sum = gather_dp(qkv_sum, near)

    part = totals.shape[1] // cols
    mine = lax.dynamic_slice_in_dim(totals, here_col * part, part, 1)
    hid = up_total.shape[0]
    return (
        output,
        grad_input,
        whole_block(qkv_sum)[0].astype(jnp.float32).reshape(w_qkv.shape),
        halves[hid:].reshape(2, wide),
        whole_block(out_sum)[0].astype(jnp.float32),
        mine[0],
        whole_block(up_sum)[0].astype(jnp.float32),
        halves[:hid],
        whole_block(down_sum)[0].astype(jnp.float32),
        mine[1],
        mine[2:4],
        mine[4:6],
    )


def solution(mesh):
    placed = (
        P(("dp", "row"), "col"),
        P(("dp", "col"), None),
        P("col", None, "row"),
        P(None, "row"),
        P("row", "col"),
        P("col"),
        P("col", "row"),
        P("row"),
        P("row", "col"),
        P("col"),
        P(None, "col"),
        P(None, "col"),
        P(("dp", "row"), "col"),
    )
    return jax.shard_map(
        shards,
        mesh=mesh,
        in_specs=placed,
        out_specs=(
            P(("dp", "row"), "col"),
            P(("dp", "row"), "col"),
            P("col", None, "row"),
            P(None, "row"),
            P("row", "col"),
            P("col"),
            P("col", "row"),
            P("row"),
            P("row", "col"),
            P("col"),
            P(None, "col"),
            P(None, "col"),
        ),
        check_vma=False,
    )
```

```python
from functools import partial
import math

import jax
import jax.numpy as jnp
from jax import lax
from jax.sharding import PartitionSpec as P

HD = 64


EPS = 1e-05


def hop(values, axis, step):
    count = lax.axis_size(axis)
    return lax.ppermute(values, axis, [(i, i ^ step) for i in range(count)])


def bit_of(axis, step):
    return (lax.axis_index(axis) & step) != 0


def in_order(mine, theirs, flag, dim):
    return jnp.stack([jnp.where(flag, theirs, mine), jnp.where(flag, mine, theirs)], dim)


def after(done, values):
    return lax.optimization_barrier((done, values))


def cut_piece(block):
    depth = block.shape[0] // lax.axis_size("dp")
    piece = lax.dynamic_slice_in_dim(block, lax.axis_index("dp") * depth, depth, 0)
    return piece.astype(jnp.bfloat16)


def gather_col(piece):
    col_count = lax.axis_size("col")
    parts = [piece] + [hop(piece, "col", k) for k in range(1, col_count)]
    step = 1
    while len(parts) > 1:
        flag = bit_of("col", step)
        parts = [in_order(parts[i], parts[i + 1], flag, 0) for i in range(0, len(parts), 2)]
        step *= 2
    return parts[0].reshape((col_count, 1) + piece.shape)


def gather_dp(held, step):
    if step == 0:
        return held
    pair = in_order(held, hop(held, "dp", step), bit_of("dp", step), 2)
    return pair.reshape((held.shape[0], held.shape[1] * 2) + held.shape[2:])


def whole_block(held):
    return held.reshape((held.shape[0], held.shape[1] * held.shape[2]) + held.shape[3:])


def cut_grad(grad):
    dp_count = lax.axis_size("dp")
    return grad.reshape((grad.shape[0], dp_count, grad.shape[1] // dp_count) + grad.shape[2:])


def halve_dp(held, step):
    pairs = held.reshape((held.shape[0], held.shape[1] // 2, 2) + held.shape[2:])
    flag = bit_of("dp", step)
    keep = jnp.where(flag, pairs[:, :, 1], pairs[:, :, 0])
    give = jnp.where(flag, pairs[:, :, 0], pairs[:, :, 1])
    got = hop(give, "dp", step)
    return (keep.astype(jnp.float32) + got.astype(jnp.float32)).astype(jnp.bfloat16)


def scatter_col(held):
    here = lax.axis_index("col")
    total = lax.dynamic_index_in_dim(held, here, 0, keepdims=False).astype(jnp.float32)
    for k in range(1, held.shape[0]):
        give = lax.dynamic_index_in_dim(held, here ^ k, 0, keepdims=False)
        total = total + hop(give, "col", k).astype(jnp.float32)
    return total.astype(jnp.bfloat16)[None]


def add_up(values, axes):
    for axis in axes:
        step = 1
        while step < lax.axis_size(axis):
            values = values + hop(values, axis, step)
            step *= 2
    return values


def from_others(values):
    count = lax.axis_size("row")
    return jnp.concatenate(
        [
            lax.ppermute(values, "row", [((i + k) % count, i) for i in range(count)])
            for k in range(1, count)
        ],
        0,
    )


def to_owners(others, mine):
    count = lax.axis_size("row")
    size = mine.shape[0]
    low = others.astype(jnp.bfloat16)
    for k in range(1, count):
        got = lax.ppermute(
            low[(k - 1) * size : k * size], "row", [(i, (i + k) % count) for i in range(count)]
        )
        mine = mine + got.astype(jnp.float32)
    return mine


def owner_perm(rows, cols, k):
    pairs = []
    for r in range(rows):
        for c in range(cols):
            owner = r * cols + (c ^ k)
            pairs.append((r * cols + c, (owner % rows) * cols + owner // rows))
    return pairs


def to_tokens(values):
    rows, cols = lax.axis_size("row"), lax.axis_size("col")
    size = values.shape[0] // cols
    blocks = values.reshape(cols, size, values.shape[1])
    here = lax.axis_index("col")
    own = lax.axis_index("col") * rows + lax.axis_index("row")
    got = []
    for k in range(cols):
        give = lax.dynamic_index_in_dim(blocks, here ^ k, 0, keepdims=False)
        got.append(lax.ppermute(give, ("row", "col"), owner_perm(rows, cols, k)))
    parts, step = got, 1
    while len(parts) > 1:
        flag = ((own % cols) & step) != 0
        parts = [
            jnp.concatenate(
                [
                    jnp.where(flag, parts[i + 1], parts[i]),
                    jnp.where(flag, parts[i], parts[i + 1]),
                ],
                1,
            )
            for i in range(0, len(parts), 2)
        ]
        step *= 2
    return parts[0]


def from_tokens(values):
    rows, cols = lax.axis_size("row"), lax.axis_size("col")
    size, width = values.shape[0], values.shape[1] // cols
    own = lax.axis_index("col") * rows + lax.axis_index("row")
    got = []
    for k in range(cols):
        start = ((own % cols) ^ k) * width
        give = lax.dynamic_slice_in_dim(values, start, width, 1)
        back = [(there, here) for here, there in owner_perm(rows, cols, k)]
        got.append(lax.ppermute(give, ("row", "col"), back))
    parts, step = got, 1
    while len(parts) > 1:
        flag = bit_of("col", step)
        parts = [
            in_order(parts[i], parts[i + 1], flag, 0).reshape((-1, width))
            for i in range(0, len(parts), 2)
        ]
        step *= 2
    return parts[0]


def gather_small(values):
    parts, step = values, 1
    while step < lax.axis_size("col"):
        pair = in_order(parts, hop(parts, "col", step), bit_of("col", step), 1)
        parts = pair.reshape(values.shape[0], -1)
        step *= 2
    return parts


def outer_blocks(first, second):
    width = second.shape[1] // lax.axis_size("col")
    return jnp.stack(
        [
            outer(first, second[:, i * width : (i + 1) * width]).astype(jnp.bfloat16)
            for i in range(lax.axis_size("col"))
        ]
    )


def norm_forward(values, gain_row, shift_row):
    center = jnp.mean(values, -1, keepdims=True)
    spread = jnp.mean(values * values, -1, keepdims=True) - center * center
    inv_std = lax.rsqrt(spread + EPS)
    normal = (values - center) * inv_std
    return (normal * gain_row + shift_row, normal, inv_std)


def norm_backward(grad_out, normal, inv_std, gain_row):
    scaled = grad_out * gain_row
    first = jnp.mean(scaled, -1, keepdims=True)
    second = jnp.mean(scaled * normal, -1, keepdims=True)
    return inv_std * (scaled - first - normal * second)


def dot(first, second):
    return jnp.dot(first, second, preferred_element_type=jnp.float32)


def dot_back(first, second):
    return jnp.einsum("tf,df->td", first, second, preferred_element_type=jnp.float32)


def outer(first, second):
    return jnp.einsum("td,tf->df", first, second, preferred_element_type=jnp.float32)


def masked_scores(query_rows, key_rows, same_seq, score_scale):
    scores = (
        jnp.einsum("qhe,khe->hqk", query_rows, key_rows, preferred_element_type=jnp.float32)
        * score_scale
    )
    return jnp.where(same_seq, scores, -1000000000.0)


def attend(query_rows, key_rows, value_rows, same_seq, score_scale):
    scores = masked_scores(query_rows, key_rows, same_seq, score_scale)
    row_max = jnp.max(scores, -1, keepdims=True)
    exp_scores = jnp.exp(scores - row_max)
    totals = jnp.sum(exp_scores, -1, keepdims=True)
    attn_probs = (exp_scores / totals).astype(jnp.bfloat16)
    context = jnp.einsum("hqk,khe->qhe", attn_probs, value_rows, preferred_element_type=jnp.float32)
    return (context, row_max + jnp.log(totals))


def attend_back(query_rows, key_rows, value_rows, same_seq, score_scale, log_total, grad_context):
    scores = masked_scores(query_rows, key_rows, same_seq, score_scale)
    attn_probs = jnp.exp(scores - log_total)
    grad_probs = jnp.einsum(
        "qhe,khe->hqk", grad_context, value_rows, preferred_element_type=jnp.float32
    )
    grad_values = jnp.einsum(
        "hqk,qhe->khe",
        attn_probs.astype(jnp.bfloat16),
        grad_context,
        preferred_element_type=jnp.float32,
    )
    inner_sum = jnp.sum(attn_probs * grad_probs, -1, keepdims=True)
    grad_scores = (attn_probs * (grad_probs - inner_sum)).astype(jnp.bfloat16)
    grad_queries = (
        jnp.einsum("hqk,khe->qhe", grad_scores, key_rows, preferred_element_type=jnp.float32)
        * score_scale
    )
    grad_keys = (
        jnp.einsum("hqk,qhe->khe", grad_scores, query_rows, preferred_element_type=jnp.float32)
        * score_scale
    )
    return (grad_queries, grad_keys, grad_values)


def shards(
    tokens,
    lengths,
    w_qkv,
    qv_bias,
    w_out,
    out_bias,
    w_up,
    up_bias,
    w_down,
    down_bias,
    norm_gain,
    norm_bias,
    cotangent,
):
    score_scale = 1.0 / math.sqrt(HD)
    gelu_exact = partial(jax.nn.gelu, approximate=False)
    rows, cols = lax.axis_size("row"), lax.axis_size("col")
    here_row, here_col = lax.axis_index("row"), lax.axis_index("col")
    wide = w_qkv.shape[2]
    far, near = lax.axis_size("dp") // 2, 1
    own_low = to_tokens(tokens.astype(jnp.bfloat16))
    qkv_held = gather_col(cut_piece(w_qkv.reshape(w_qkv.shape[0], 3 * wide)))
    small = jnp.stack(
        [out_bias, down_bias, norm_gain[0], norm_gain[1], norm_bias[0], norm_bias[1]]
    )
    small = gather_small(small)
    other_low = from_others(own_low)
    pieces = jnp.concatenate([cut_piece(w_out), cut_piece(w_down)], 0)
    (qkv_held, own_low), pieces = after((qkv_held, own_low), pieces)
    pair_held = gather_col(pieces)
    qkv_held, piece_up = after(gather_dp(qkv_held, far), cut_piece(w_up))
    up_held = gather_col(piece_up)
    qkv_held, pair_held = after(gather_dp(qkv_held, near), pair_held)
    w_qkv_all = whole_block(qkv_held).reshape(-1, 3 * wide)
    pair_held = gather_dp(pair_held, far)
    out_bias_all, down_bias_all = small[0], small[1]
    gains, shifts = small[2:4], small[4:6]

    size = own_low.shape[0]
    full_bias = jnp.concatenate([qv_bias[0], jnp.zeros_like(qv_bias[0]), qv_bias[1]])
    qkv = jnp.concatenate(
        [
            (dot(own_low, w_qkv_all) + full_bias).astype(jnp.bfloat16),
            (dot(other_low, w_qkv_all) + full_bias).astype(jnp.bfloat16),
        ],
        0,
    )
    qkv, (pair_held, up_held) = after(qkv, (pair_held, up_held))
    pair_held, up_held = gather_dp(pair_held, near), gather_dp(up_held, far)
    length = qkv.shape[0]
    head_count = wide // HD
    qkv = qkv.reshape(length, 3, head_count, HD)
    query_rows, key_rows, value_rows = qkv[:, 0], qkv[:, 1], qkv[:, 2]
    seq_ends = jnp.cumsum(lengths[0])
    positions = (jnp.arange(length, dtype=jnp.int32) + here_row * size) % length
    segment = jnp.sum((positions[:, None] >= seq_ends[None, :]).astype(jnp.int32), -1)
    same_seq = (segment[:, None] == segment[None, :])[None]
    context, log_total = attend(query_rows, key_rows, value_rows, same_seq, score_scale)
    context = context.reshape(length, wide).astype(jnp.bfloat16)
    context, (pair_held, up_held) = after(context, (pair_held, up_held))
    cut = w_out.shape[0] // lax.axis_size("dp")
    w_out_all = whole_block(pair_held[:, :, :cut]).transpose(1, 0, 2).reshape(w_out.shape[0], -1)
    up_held = gather_dp(up_held, near)
    attn_other = dot(context[size:], w_out_all)
    attn_out = to_owners(attn_other, dot(context[:size], w_out_all)) + out_bias_all
    normed_one, normal_one, inv_one = norm_forward(own_low.astype(jnp.float32) + attn_out, gains[0], shifts[0])
    normed_own = normed_one.astype(jnp.bfloat16)
    normed_other = from_others(normed_own)
    w_up_all = whole_block(up_held).reshape(-1, w_up.shape[1])
    w_down_all = whole_block(pair_held[:, :, cut:]).transpose(1, 0, 2).reshape(w_down.shape[0], -1)
    pre_own = dot(normed_own, w_up_all) + up_bias
    pre_own, cotangent_low = after(pre_own, cotangent.astype(jnp.bfloat16))
    own_cotangent = to_tokens(cotangent_low).astype(jnp.float32)
    pre_other = dot(normed_other, w_up_all) + up_bias
    hidden_own = gelu_exact(pre_own).astype(jnp.bfloat16)
    hidden_other = gelu_exact(pre_other).astype(jnp.bfloat16)
    hidden = jnp.concatenate([hidden_own, hidden_other], 0)
    mlp_other = dot(hidden_other, w_down_all)
    mlp_out = to_owners(mlp_other, dot(hidden_own, w_down_all)) + down_bias_all
    last, normal_two, inv_two = norm_forward(normed_one + mlp_out, gains[1], shifts[1])
    grad_last = norm_backward(own_cotangent, normal_two, inv_two, gains[1])
    gain_two = jnp.sum(own_cotangent * normal_two, 0)
    shift_two = jnp.sum(own_cotangent, 0)
    mlp_grad_own = grad_last.astype(jnp.bfloat16)
    mlp_grad_other = from_others(mlp_grad_own)
    down_total = jnp.sum(mlp_grad_own, 0, dtype=jnp.float32)
    mlp_grad_own, last = after(mlp_grad_own, last)
    output = from_tokens(last.astype(jnp.bfloat16)).astype(jnp.float32)
    down_sum = cut_grad(outer_blocks(hidden, jnp.concatenate([mlp_grad_own, mlp_grad_other], 0)))
    down_sum = halve_dp(down_sum, near)
    pre_grad_own = jax.vjp(gelu_exact, pre_own)[1](dot_back(mlp_grad_own, w_down_all))[0]
    pre_grad_own = pre_grad_own.astype(jnp.bfloat16)
    pre_grad_other = jax.vjp(gelu_exact, pre_other)[1](dot_back(mlp_grad_other, w_down_all))[0]
    pre_grad_other = pre_grad_other.astype(jnp.bfloat16)
    pre_grad_other, down_sum = after(pre_grad_other, down_sum)
    down_sum = halve_dp(down_sum, far)
    normed_part = dot_back(pre_grad_other, w_up_all)
    grad_normed = to_owners(normed_part, dot_back(pre_grad_own, w_up_all)) + grad_last
    pre_grad = jnp.concatenate([pre_grad_own, pre_grad_other], 0)
    up_total = jnp.sum(pre_grad, 0, dtype=jnp.float32)
    up_grad = outer(jnp.concatenate([normed_own, normed_other], 0), pre_grad).astype(jnp.bfloat16)
    up_sum = halve_dp(cut_grad(up_grad.reshape((cols,) + w_up.shape)), near)
    grad_middle = norm_backward(grad_normed, normal_one, inv_one, gains[0])
    gain_one = jnp.sum(grad_normed * normal_one, 0)
    shift_one = jnp.sum(grad_normed, 0)
    attn_grad_own = grad_middle.astype(jnp.bfloat16)
    attn_grad_own, (down_sum, up_sum) = after(attn_grad_own, (down_sum, up_sum))
    attn_grad_other = from_others(attn_grad_own)
    down_sum = scatter_col(down_sum)
    up_sum = halve_dp(up_sum, far)
    out_total = jnp.sum(attn_grad_own, 0, dtype=jnp.float32)
    totals = add_up(
        jnp.stack([out_total, down_total, gain_one, gain_two, shift_one, shift_two]),
        ("row",),
    )
    grad_context = jnp.concatenate(
        [
            dot_back(attn_grad_own, w_out_all).astype(jnp.bfloat16),
            dot_back(attn_grad_other, w_out_all).astype(jnp.bfloat16),
        ],
        0,
    ).reshape(length, head_count, HD)
    attn_grad = jnp.concatenate([attn_grad_own, attn_grad_other], 0)
    out_sum = halve_dp(cut_grad(outer_blocks(context, attn_grad)), near)
    grad_queries, grad_keys, grad_values = attend_back(
        query_rows, key_rows, value_rows, same_seq, score_scale, log_total, grad_context
    )
    grad_qkv = (
        jnp.stack([grad_queries, grad_keys, grad_values], 1)
        .reshape(length, 3 * wide)
        .astype(jnp.bfloat16)
    )
    grad_qkv, (down_sum, up_sum, out_sum) = after(grad_qkv, (down_sum, up_sum, out_sum))
    qkv_totals = jnp.sum(grad_qkv, 0, dtype=jnp.float32)
    qkv_grad = outer(jnp.concatenate([own_low, other_low], 0), grad_qkv).astype(jnp.bfloat16)
    qkv_sum = halve_dp(cut_grad(qkv_grad.reshape(cols, -1, 3 * wide)), near)
    out_sum = halve_dp(out_sum, far)
    up_sum = scatter_col(up_sum)
    down_sum = gather_dp(down_sum, far)
    input_other = dot_back(grad_qkv[size:], w_qkv_all)
    grad_own = to_owners(input_other, dot_back(grad_qkv[:size], w_qkv_all)) + grad_middle
    qkv_sum, (out_sum, up_sum, down_sum, grad_own) = after(
        qkv_sum, (out_sum, up_sum, down_sum, grad_own)
    )
    qkv_sum = halve_dp(qkv_sum, far)
    grad_input = from_tokens(grad_own.astype(jnp.bfloat16)).astype(jnp.float32)
    out_sum = scatter_col(out_sum)
    up_sum = gather_dp(up_sum, far)
    down_sum = gather_dp(down_sum, near)
    qkv_sum, (out_sum, up_sum) = after(qkv_sum, (out_sum, up_sum))
    qkv_sum = scatter_col(qkv_sum)
    out_sum = gather_dp(out_sum, far)
    up_sum = gather_dp(up_sum, near)
    qkv_sum, out_sum = after(qkv_sum, out_sum)
    qkv_sum = gather_dp(qkv_sum, far)
    out_sum = gather_dp(out_sum, near)
    qkv_sum = gather_dp(qkv_sum, near)

    sums = jnp.concatenate(
        [totals.reshape(-1), up_total, qkv_totals[:wide], qkv_totals[2 * wide :]]
    )
    sums = add_up(sums.reshape(-1, 128), ("dp", "col")).reshape(-1)
    halves = sums[totals.size :]
    totals = sums[: totals.size].reshape(totals.shape)
    part = totals.shape[1] // cols
    mine = lax.dynamic_slice_in_dim(totals, here_col * part, part, 1)
    hid = up_total.shape[0]
    return (
        output,
        grad_input,
        whole_block(qkv_sum)[0].astype(jnp.float32).reshape(w_qkv.shape),
        halves[hid:].reshape(2, wide),
        whole_block(out_sum)[0].astype(jnp.float32),
        mine[0],
        whole_block(up_sum)[0].astype(jnp.float32),
        halves[:hid],
        whole_block(down_sum)[0].astype(jnp.float32),
        mine[1],
        mine[2:4],
        mine[4:6],
    )


def solution(mesh):
    placed = (
        P(("dp", "row"), "col"),
        P(("dp", "col"), None),
        P("col", None, "row"),
        P(None, "row"),
        P("row", "col"),
        P("col"),
        P("col", "row"),
        P("row"),
        P("row", "col"),
        P("col"),
        P(None, "col"),
        P(None, "col"),
        P(("dp", "row"), "col"),
    )
    return jax.shard_map(
        shards,
        mesh=mesh,
        in_specs=placed,
        out_specs=(
            P(("dp", "row"), "col"),
            P(("dp", "row"), "col"),
            P("col", None, "row"),
            P(None, "row"),
            P("row", "col"),
            P("col"),
            P("col", "row"),
            P("row"),
            P("row", "col"),
            P("col"),
            P(None, "col"),
            P(None, "col"),
        ),
        check_vma=False,
    )
```
